1024 devices in a mesh: dp: 32 (over x_lo, z), mx: 4 (over x_hi, core), my: 8 (over y).
Axes of the slice: x: 4 (x_hi: 2, x_lo: 2; x = x_hi * 2 + x_lo), y: 8, z: 16, core: 2. Of those that a mesh axis runs over, the one named last changes fastest.
Arguments:
- tokens_in: bfloat16 [8192, 6144], P('dp', 'mx'), as said below
- norm_gain: float32 [6144], P('mx'), may hold values from 0.1 to 1.9
- in_weight: bfloat16 [6144, 12288], P('mx', 'my'), as said below
- cotangent: bfloat16 [8192, 12288], P('dp', 'my'), may hold values from -6 to 6
Outputs:
- grad_weight: bfloat16 [4, 32, 48, 12288], P('mx', 'dp', None, 'my')
- grad_tokens: bfloat16 [8192, 6144], P(('dp', 'my'), 'mx')
The draws below stay inside these ranges and needn't reach their ends.
Inputs may be any that keep to these rules, and one draw needn't show every extreme that they name: `tokens_in`: Real-valued activations; no structure is promised. `in_weight`: Real-valued weights; no structure is promised.
All inputs are finite; a program needn't handle non-finite values.
Results may differ from the reference program's by a relative error of at most 0.034.
Values may be sent and summed in bfloat16 or wider, within the bound.
No kernel may reach another device: no remote copies, remote signals or barrier semaphores. Data moves between devices by JAX's collectives and lax.ppermute only.
A program may use at most 32 MiB of HBM per device.

```python
import math
import jax
import jax.numpy as jnp
from jax import lax

D = 6144
F = 12288
TOK_DEV = 256
TOKENS = 8192
DROW = 48
N_DP = 32
N_MX = 4


def draw_tokens_in(key, part):
    key = jax.random.fold_in(key, 11)
    key_base, key_row, key_col = jax.random.split(key, 3)
    base = jnp.clip(jax.random.normal(key_base, (TOKENS, D), jnp.float32), -4.0, 4.0)
    row_scale = jnp.exp(jax.random.uniform(key_row, (TOKENS, 1), jnp.float32) * math.log(10.0))
    col_scale = jnp.exp(jax.random.uniform(key_col, (1, D), jnp.float32) * math.log(10.0))
    ramp = 1.0 + 2.0 * jnp.arange(D, dtype=jnp.float32)[None, :] / D
    return (base * row_scale * col_scale * ramp * 0.1).astype(jnp.bfloat16)


def weight_rows(key, rise):
    key_noise, key_rough, key_col = jax.random.split(key, 3)
    noise = jnp.clip(jax.random.normal(key_noise, (D, F), jnp.float32), -5.0, 5.0)
    rough = jax.random.uniform(key_rough, (D, 1), jnp.float32, 0.5, 1.5)
    position = jnp.arange(D, dtype=jnp.float32)[:, None] / D
    row_factor = 0.35 * jnp.exp(position * math.log(rise)) * rough
    col_factor = jnp.clip(jax.random.normal(key_col, (1, F), jnp.float32), -4.0, 4.0)
    return (noise + row_factor * col_factor) * (1.0 / math.sqrt(D))


def draw_in_weight(key, part):
    key = jax.random.fold_in(key, 23)
    full = weight_rows(key, 8.0)
    return full.astype(jnp.bfloat16)


def spiked(values, stream_key, source, target, blocks, factor):
    owner, partner = [(jnp.arange(values.shape[dim]) // (values.shape[dim] // blocks)).reshape([-1 if axis == dim else 1 for axis in range(values.ndim)]) for dim in (source, target)]
    chosen = jax.random.permutation(stream_key, blocks)[partner]
    strong = (owner == chosen) | (owner == (partner + blocks // 2) % blocks)
    return jnp.where(strong, factor * values, values)


def shard_levels(stream_key, dims, pieces, least, largest):
    def one(dim, parts):
        heights = jax.random.uniform(jax.random.fold_in(jax.random.fold_in(stream_key, 6), dim), (parts,), jnp.float32, least / len(pieces), largest / len(pieces))
        return jnp.repeat(jnp.exp(heights), dims[dim] // parts).reshape((-1,) + (1,) * (len(dims) - dim - 1))

    gain = one(*pieces[0])
    for cut in pieces[1:]:
        gain = gain * one(*cut)
    return gain


def noise_with(key, dims, spread, limit, pieces, heavy, kind=jnp.bfloat16):
    values = spread * jax.random.normal(key, dims, jnp.float32)
    if pieces:
        values = values * shard_levels(key, dims, pieces, -0.22, 0.18)
    return jnp.clip(spiked(values, jax.random.fold_in(key, 3), *heavy), -limit, limit).astype(kind)


def setup_inputs(seed: int = 0) -> dict:
    keys = jax.random.split(jax.random.key(seed), 5)
    return {
        "tokens_in": draw_tokens_in(jax.random.fold_in(keys[4], 71), 0),
        "norm_gain": jnp.clip(1.0 + 0.18 * jax.random.normal(keys[1], (D,), jnp.float32), 0.1, 1.9),
        "in_weight": draw_in_weight(jax.random.fold_in(keys[4], 71), 0),
        "cotangent": noise_with(keys[3], (TOKENS, F), 1.0, 6.0, ((0, 32), (1, 8)), (0, 1, 32, 2.75)),
    }


epsilon = 1e-06

def gelu_slope(pre):
    cdf = 0.5 * (1.0 + jax.scipy.special.erf(pre * (1.0 / math.sqrt(2.0))))
    return cdf + pre * jnp.exp(-0.5 * pre * pre) * (1.0 / math.sqrt(2.0 * math.pi))

def reference(tokens_in, norm_gain, in_weight, cotangent):
    values = tokens_in.astype(jnp.float32)
    row_mean = lax.optimization_barrier(jnp.sum(values, axis=1)) / D
    mean_sq = lax.optimization_barrier(jnp.sum(values * values, axis=1)) / D
    inv_std = lax.rsqrt(mean_sq - row_mean * row_mean + epsilon)
    centred = (values - row_mean[:, None]) * inv_std[:, None]
    normed = (centred * norm_gain[None, :]).astype(jnp.bfloat16)
    pre = jnp.dot(normed, in_weight, preferred_element_type=jnp.float32)
    dpre = (cotangent.astype(jnp.float32) * gelu_slope(pre)).astype(jnp.bfloat16)
    grad_scale = 1.0 / math.sqrt(TOKENS)
    normed_groups = normed.reshape(N_DP, TOK_DEV, D)
    dpre_groups = dpre.reshape(N_DP, TOK_DEV, F)

    def accumulate(total, pair):
        term = jnp.dot(pair[0].T, pair[1], preferred_element_type=jnp.float32) * grad_scale
        return (total + term.astype(jnp.bfloat16).astype(jnp.float32), None)
    total, unused = lax.scan(accumulate, jnp.zeros((D, F), jnp.float32), (normed_groups, dpre_groups))
    grad_weight = total.astype(jnp.bfloat16).reshape(N_MX, N_DP, DROW, F)
    dnormed = jnp.dot(dpre, in_weight.T, preferred_element_type=jnp.float32)
    dcentred = dnormed * norm_gain[None, :]
    mean_a = lax.optimization_barrier(jnp.sum(dcentred, axis=1)) / D
    mean_b = lax.optimization_barrier(jnp.sum(dcentred * centred, axis=1)) / D
    grad_tokens = inv_std[:, None] * (dcentred - mean_a[:, None] - centred * mean_b[:, None])
    return (grad_weight, grad_tokens.astype(jnp.bfloat16))
```

```python
import math

import jax
import jax.numpy as jnp
from jax import lax
from jax.sharding import PartitionSpec as P

epsilon = 1e-06
BF = jnp.bfloat16
F32 = jnp.float32


def gelu_slope(pre):
    cdf = 0.5 * (1.0 + jax.scipy.special.erf(pre * (1.0 / math.sqrt(2.0))))
    return cdf + pre * jnp.exp(-0.5 * pre * pre) * (1.0 / math.sqrt(2.0 * math.pi))


def swap(value, axis, size, bits):
    return lax.ppermute(value, axis, [(i, i ^ bits) for i in range(size)])


def rows_at(value, start, count):
    return lax.dynamic_slice_in_dim(value, start, count, 0)


def dot(a, b, dims=((1,), (0,))):
    return lax.dot_general(a, b, (dims, ((), ())), preferred_element_type=F32)


Z = 16
ZH = Z // 2
GROUP = (16, 1, 17)


def body(tokens_in, norm_gain, in_weight, cotangent):
    tok_rows, width = tokens_in.shape
    hidden = in_weight.shape[1]
    n_dp, n_mx, n_my = lax.axis_size("dp"), lax.axis_size("mx"), lax.axis_size("my")
    d_all = width * n_mx
    half = tok_rows // 2
    dp, my = lax.axis_index("dp"), lax.axis_index("my")
    core = lax.axis_index("mx") % 2
    zh, x_lo, zl = (dp % Z) // 2, dp // Z, dp % 2
    block = width // n_dp

    values = tokens_in.astype(F32)
    sum_one, sum_two = lax.psum((jnp.sum(values, axis=1), jnp.sum(values * values, axis=1)), "mx")
    row_mean = sum_one / d_all
    inv_std = lax.rsqrt(sum_two / d_all - row_mean * row_mean + epsilon)
    centred = (values - row_mean[:, None]) * inv_std[:, None]
    normed = (centred * norm_gain[None, :]).astype(BF)

    mine = rows_at(normed, core * half, half)
    other = rows_at(normed, (1 - core) * half, half)
    sent = dot(other, in_weight).astype(BF)
    from_core = swap(sent, "mx", n_mx, 1)
    kept = dot(mine, in_weight) + from_core.astype(F32)
    from_x = swap(kept.astype(BF), "mx", n_mx, 2)
    pre = kept + from_x.astype(F32)
    cot = rows_at(cotangent, core * half, half)
    dpre = (cot.astype(F32) * gelu_slope(pre)).astype(BF)

    turned = jnp.concatenate([mine.T, other.T], axis=1).reshape(2, ZH, 2, block, tok_rows)
    turned = jnp.concatenate([turned, turned], axis=1)

    def columns(xb, zb):
        piece = lax.dynamic_slice(
            turned, (x_lo ^ xb, zh, zl ^ zb, 0, 0), (1, ZH, 1, block, tok_rows)
        )
        return piece.reshape(ZH * block, tok_rows)

    left = [columns(0, 0)]
    for bits in GROUP:
        left.append(swap(columns(bits // 16, bits % 2), "dp", n_dp, bits))

    own_pair = swap(dpre, "mx", n_mx, 1)
    arrived = [swap(dpre, "dp", n_dp, bits) for bits in GROUP]

    dpre_own = jnp.concatenate([dpre, own_pair], axis=0)
    back = dot(dpre_own, in_weight, ((1,), (1,))).astype(BF)
    own_rows = tok_rows // n_my
    parts = []
    for step in range(n_my):
        owner = (my + step) % n_my
        part = rows_at(back, (owner * own_rows + core * half) % tok_rows, own_rows)
        if step:
            part = lax.ppermute(part, "my", [(i, (i + step) % n_my) for i in range(n_my)])
        parts.append(part.astype(F32))
    dnormed = sum(parts)

    arrived = jnp.concatenate(arrived, axis=0)
    paired = swap(arrived, "mx", n_mx, 1)
    right = [dpre_own]
    for i in range(len(GROUP)):
        right.append(arrived[i * half : (i + 1) * half])
        right.append(paired[i * half : (i + 1) * half])
    grad_scale = 1.0 / math.sqrt(n_dp * tok_rows)
    term = (dot(jnp.concatenate(left, axis=1), jnp.concatenate(right, axis=0)) * grad_scale).astype(BF)
    total = term[:block].astype(F32)
    for step in range(1, ZH):
        perm = [
            (i, i // Z * Z + (i % Z + 2 * step) % Z) for i in range(n_dp)
        ]
        total += lax.ppermute(term[step * block : (step + 1) * block], "dp", perm).astype(F32)
    grad_weight = total.astype(BF).reshape(1, 1, block, hidden)

    first_row = my * own_rows
    centred_rows = rows_at(centred, first_row, own_rows)
    inv_rows = rows_at(inv_std, first_row, own_rows)
    dcentred = dnormed * norm_gain[None, :]
    total_a, total_b = lax.psum(
        (jnp.sum(dcentred, axis=1), jnp.sum(dcentred * centred_rows, axis=1)), "mx"
    )
    grad_tokens = inv_rows[:, None] * (
        dcentred - total_a[:, None] / d_all - centred_rows * (total_b[:, None] / d_all)
    )
    return (grad_weight, grad_tokens.astype(BF))


def solution(mesh):
    return jax.shard_map(
        body,
        mesh=mesh,
        in_specs=(P("dp", "mx"), P("mx"), P("mx", "my"), P("dp", "my")),
        out_specs=(P("mx", "dp", None, "my"), P(("dp", "my"), "mx")),
        check_vma=False,
    )
```

```python
import math

import jax
import jax.numpy as jnp
from jax import lax
from jax.experimental import pallas as pl
from jax.experimental.pallas import tpu as pltpu
from jax.sharding import PartitionSpec as P

epsilon = 1e-06
BF = jnp.bfloat16
F32 = jnp.float32


def gelu_slope(pre):
    cdf = 0.5 * (1.0 + jax.scipy.special.erf(pre * (1.0 / math.sqrt(2.0))))
    return cdf + pre * jnp.exp(-0.5 * pre * pre) * (1.0 / math.sqrt(2.0 * math.pi))


def swap(value, axis, size, bits):
    return lax.ppermute(value, axis, [(i, i ^ bits) for i in range(size)])


def rows_at(value, start, count):
    return lax.dynamic_slice_in_dim(value, start, count, 0)


def dot(a, b, dims=((1,), (0,))):
    return lax.dot_general(a, b, (dims, ((), ())), preferred_element_type=F32)


def weight_kernel(scale, rows, *refs):
    left, right, out = refs[:4], refs[4:12], refs[12:]
    hidden = right[0].shape[1]
    tile = 256

    @pl.loop(0, hidden // tile)
    def _(step):
        cols = pl.ds(pl.multiple_of(step * tile, tile), tile)
        total = None
        for i in range(4):
            tokens = jnp.concatenate([right[2 * i][:, cols], right[2 * i + 1][:, cols]], axis=0)
            term = dot(left[i][...], tokens)
            total = term if total is None else total + term
        total = (total * scale).astype(BF)
        for i, ref in enumerate(out):
            ref[:, cols] = total[i * rows : (i + 1) * rows]


def weight_blocks(left, right, scale, rows):
    count = left[0].shape[0] // rows
    hidden = right[0].shape[1]
    tokens = sum(r.shape[0] for r in right)
    whole = pl.BlockSpec(memory_space=pltpu.VMEM)
    return pl.pallas_call(
        lambda *refs: weight_kernel(scale, rows, *refs),
        out_shape=[jax.ShapeDtypeStruct((rows, hidden), BF)] * count,
        in_specs=[whole] * (len(left) + len(right)),
        out_specs=[whole] * count,
        compiler_params=pltpu.CompilerParams(vmem_limit_bytes=8 * 1024 * 1024),
        cost_estimate=pl.CostEstimate(
            flops=2 * rows * count * tokens * hidden,
            bytes_accessed=2 * (rows * count * (tokens + hidden) + tokens * hidden),
            transcendentals=0,
        ),
    )(*left, *right)


Z = 16
ZH = Z // 2
GROUP = (16, 1, 17)


def body(tokens_in, norm_gain, in_weight, cotangent):
    tok_rows, width = tokens_in.shape
    hidden = in_weight.shape[1]
    n_dp, n_mx, n_my = lax.axis_size("dp"), lax.axis_size("mx"), lax.axis_size("my")
    d_all = width * n_mx
    half = tok_rows // 2
    dp, my = lax.axis_index("dp"), lax.axis_index("my")
    core = lax.axis_index("mx") % 2
    zh, x_lo, zl = (dp % Z) // 2, dp // Z, dp % 2
    block = width // n_dp

    values = tokens_in.astype(F32)
    sum_one, sum_two = lax.psum((jnp.sum(values, axis=1), jnp.sum(values * values, axis=1)), "mx")
    row_mean = sum_one / d_all
    inv_std = lax.rsqrt(sum_two / d_all - row_mean * row_mean + epsilon)
    centred = (values - row_mean[:, None]) * inv_std[:, None]
    normed = (centred * norm_gain[None, :]).astype(BF)

    mine = rows_at(normed, core * half, half)
    other = rows_at(normed, (1 - core) * half, half)
    sent = dot(other, in_weight).astype(BF)
    from_core = swap(sent, "mx", n_mx, 1)
    kept = lax.optimization_barrier(dot(mine, in_weight)) + from_core.astype(F32)
    from_x = swap(kept.astype(BF), "mx", n_mx, 2)

    turned = jnp.concatenate([mine.T, other.T], axis=1).reshape(2, ZH, 2, block, tok_rows)
    turned = jnp.concatenate([turned, turned], axis=1)

    def columns(xb, zb):
        piece = lax.dynamic_slice(
            turned, (x_lo ^ xb, zh, zl ^ zb, 0, 0), (1, ZH, 1, block, tok_rows)
        )
        return piece.reshape(ZH * block, tok_rows)

    left = [columns(0, 0)]
    for bits in GROUP:
        left.append(swap(columns(bits // 16, bits % 2), "dp", n_dp, bits))
    from_x, *left = lax.optimization_barrier((from_x, *left))

    pre = kept + from_x.astype(F32)
    cot = rows_at(cotangent, core * half, half)
    dpre = (cot.astype(F32) * gelu_slope(pre)).astype(BF)

    own_pair = swap(dpre, "mx", n_mx, 1)
    right = [dpre, own_pair]
    arrived = [swap(dpre, "dp", n_dp, bits) for bits in GROUP]

    in_order = jnp.where(core == 0, jnp.concatenate(right, axis=0), jnp.concatenate(right[::-1], axis=0))
    back = dot(in_order, in_weight, ((1,), (1,)))
    back, *arrived = lax.optimization_barrier((back, *arrived))
    dnormed = lax.psum_scatter(back, "my", scatter_dimension=0, tiled=True)
    own_rows = tok_rows // n_my

    for piece in arrived:
        right += [piece, swap(piece, "mx", n_mx, 1)]
    terms = weight_blocks(left, right, 1.0 / math.sqrt(n_dp * tok_rows), block)

    def hop(value, way):
        perm = [(i, i // Z * Z + (i + 2 * way) % Z) for i in range(n_dp)]
        return lax.ppermute(value.astype(BF), "dp", perm).astype(F32)

    ahead, behind = terms[ZH // 2], terms[ZH // 2 + 1]
    for step in range(1, ZH // 2):
        ahead = hop(ahead, 1) + terms[ZH // 2 - step].astype(F32)
        behind = hop(behind, -1) + terms[(ZH // 2 + 1 + step) % ZH].astype(F32)
    ahead, dnormed = lax.optimization_barrier((ahead, dnormed))
    grad_weight = (behind + hop(ahead, 1)).astype(BF).reshape(1, 1, block, hidden)

    first_row = my * own_rows
    centred_rows = rows_at(centred, first_row, own_rows)
    inv_rows = rows_at(inv_std, first_row, own_rows)
    dcentred = dnormed * norm_gain[None, :]
    total_a, total_b = lax.psum(
        (jnp.sum(dcentred, axis=1), jnp.sum(dcentred * centred_rows, axis=1)), "mx"
    )
    grad_tokens = inv_rows[:, None] * (
        dcentred - total_a[:, None] / d_all - centred_rows * (total_b[:, None] / d_all)
    )
    return (grad_weight, grad_tokens.astype(BF))


def solution(mesh):
    return jax.shard_map(
        body,
        mesh=mesh,
        in_specs=(P("dp", "mx"), P("mx"), P("mx", "my"), P("dp", "my")),
        out_specs=(P("mx", "dp", None, "my"), P(("dp", "my"), "mx")),
        check_vma=False,
    )
```

```python
import math

import jax
import jax.numpy as jnp
from jax import lax
from jax.experimental import pallas as pl
from jax.experimental.pallas import tpu as pltpu
from jax.sharding import PartitionSpec as P

epsilon = 1e-06
BF = jnp.bfloat16
F32 = jnp.float32


def gelu_slope(pre):
    cdf = 0.5 * (1.0 + jax.scipy.special.erf(pre * (1.0 / math.sqrt(2.0))))
    return cdf + pre * jnp.exp(-0.5 * pre * pre) * (1.0 / math.sqrt(2.0 * math.pi))


def swap(value, axis, size, bits):
    return lax.ppermute(value, axis, [(i, i ^ bits) for i in range(size)])


def rows_at(value, start, count):
    return lax.dynamic_slice_in_dim(value, start, count, 0)


def dot(a, b, dims=((1,), (0,))):
    return lax.dot_general(a, b, (dims, ((), ())), preferred_element_type=F32)


def weight_kernel(scale, rows, *refs):
    left, right, out = refs[:4], refs[4:12], refs[12:]
    hidden = right[0].shape[1]
    tile = 256

    @pl.loop(0, hidden // tile)
    def _(step):
        cols = pl.ds(pl.multiple_of(step * tile, tile), tile)
        total = None
        for i in range(4):
            tokens = jnp.concatenate([right[2 * i][:, cols], right[2 * i + 1][:, cols]], axis=0)
            term = dot(left[i][...], tokens)
            total = term if total is None else total + term
        total = (total * scale).astype(BF)
        for i, ref in enumerate(out):
            ref[:, cols] = total[i * rows : (i + 1) * rows]


def weight_blocks(left, right, scale, rows):
    count = left[0].shape[0] // rows
    hidden = right[0].shape[1]
    tokens = sum(r.shape[0] for r in right)
    whole = pl.BlockSpec(memory_space=pltpu.VMEM)
    return pl.pallas_call(
        lambda *refs: weight_kernel(scale, rows, *refs),
        out_shape=[jax.ShapeDtypeStruct((rows, hidden), BF)] * count,
        in_specs=[pl.BlockSpec()] * len(left) + [whole] * len(right),
        out_specs=[whole] * count,
        compiler_params=pltpu.CompilerParams(vmem_limit_bytes=8 * 1024 * 1024),
        cost_estimate=pl.CostEstimate(
            flops=2 * rows * count * tokens * hidden,
            bytes_accessed=2 * (rows * count * (tokens + hidden) + tokens * hidden),
            transcendentals=0,
        ),
    )(*left, *right)


Z = 16
ZH = Z // 2
GROUP = (16, 1, 17)


def body(tokens_in, norm_gain, in_weight, cotangent):
    tok_rows, width = tokens_in.shape
    hidden = in_weight.shape[1]
    n_dp, n_mx, n_my = lax.axis_size("dp"), lax.axis_size("mx"), lax.axis_size("my")
    d_all = width * n_mx
    half = tok_rows // 2
    dp, my = lax.axis_index("dp"), lax.axis_index("my")
    core = lax.axis_index("mx") % 2
    zh, x_lo, zl = (dp % Z) // 2, dp // Z, dp % 2
    block = width // n_dp

    values = tokens_in.astype(F32)
    sum_one, sum_two = lax.psum((jnp.sum(values, axis=1), jnp.sum(values * values, axis=1)), "mx")
    row_mean = sum_one / d_all
    inv_std = lax.rsqrt(sum_two / d_all - row_mean * row_mean + epsilon)
    centred = (values - row_mean[:, None]) * inv_std[:, None]
    normed = (centred * norm_gain[None, :]).astype(BF)

    mine = rows_at(normed, core * half, half)
    other = rows_at(normed, (1 - core) * half, half)
    sent = dot(other, in_weight).astype(BF)
    from_core = swap(sent, "mx", n_mx, 1)
    kept = lax.optimization_barrier(dot(mine, in_weight)) + from_core.astype(F32)
    from_x = swap(kept.astype(BF), "mx", n_mx, 2)

    turned = jnp.concatenate([mine.T, other.T], axis=1).reshape(2, ZH, 2, block, tok_rows)
    turned = jnp.concatenate([turned, turned], axis=1)

    def columns(xb, zb):
        piece = lax.dynamic_slice(
            turned, (x_lo ^ xb, zh, zl ^ zb, 0, 0), (1, ZH, 1, block, tok_rows)
        )
        return piece.reshape(ZH * block, tok_rows)

    left = [columns(0, 0)]
    for bits in GROUP:
        left.append(columns(bits // 16, bits % 2))
    from_x, *left = lax.optimization_barrier((from_x, *left))

    pre = kept + from_x.astype(F32)
    cot = rows_at(cotangent, core * half, half)
    dpre = (cot.astype(F32) * gelu_slope(pre)).astype(BF)

    own_pair = swap(dpre, "mx", n_mx, 1)
    right = [dpre, own_pair]
    arrived = [swap(dpre, "dp", n_dp, bits) for bits in GROUP]

    in_order = jnp.where(core == 0, jnp.concatenate(right, axis=0), jnp.concatenate(right[::-1], axis=0))
    back = dot(in_order, in_weight, ((1,), (1,)))
    back, *left = lax.optimization_barrier((back, *left))
    left[1:] = [swap(piece, "dp", n_dp, bits) for piece, bits in zip(left[1:], GROUP)]
    arrived[2], *left = lax.optimization_barrier((arrived[2], *left))
    dnormed = lax.psum_scatter(back, "my", scatter_dimension=0, tiled=True)
    own_rows = tok_rows // n_my

    for piece in arrived:
        right += [piece, swap(piece, "mx", n_mx, 1)]
    terms = weight_blocks(left, right, 1.0 / math.sqrt(n_dp * tok_rows), block)

    def hop(value, way):
        perm = [(i, i // Z * Z + (i + 2 * way) % Z) for i in range(n_dp)]
        return lax.ppermute(value.astype(BF), "dp", perm).astype(F32)

    ahead, behind = terms[ZH // 2], terms[ZH // 2 + 1]
    for step in range(1, ZH // 2):
        ahead = hop(ahead, 1) + terms[ZH // 2 - step].astype(F32)
        behind = hop(behind, -1) + terms[(ZH // 2 + 1 + step) % ZH].astype(F32)
    ahead, dnormed = lax.optimization_barrier((ahead, dnormed))
    grad_weight = (behind + hop(ahead, 1)).astype(BF).reshape(1, 1, block, hidden)

    first_row = my * own_rows
    centred_rows = rows_at(centred, first_row, own_rows)
    inv_rows = rows_at(inv_std, first_row, own_rows)
    dcentred = dnormed * norm_gain[None, :]
    total_a, total_b = lax.psum(
        (jnp.sum(dcentred, axis=1), jnp.sum(dcentred * centred_rows, axis=1)), "mx"
    )
    grad_tokens = inv_rows[:, None] * (
        dcentred - total_a[:, None] / d_all - centred_rows * (total_b[:, None] / d_all)
    )
    return (grad_weight, grad_tokens.astype(BF))


def solution(mesh):
    return jax.shard_map(
        body,
        mesh=mesh,
        in_specs=(P("dp", "mx"), P("mx"), P("mx", "my"), P("dp", "my")),
        out_specs=(P("mx", "dp", None, "my"), P(("dp", "my"), "mx")),
        check_vma=False,
    )
```

```python
import math

import jax
import jax.numpy as jnp
from jax import lax
from jax.experimental import pallas as pl
from jax.experimental.pallas import tpu as pltpu
from jax.sharding import PartitionSpec as P

epsilon = 1e-06
BF = jnp.bfloat16
F32 = jnp.float32


def gelu_slope(pre):
    cdf = 0.5 * (1.0 + jax.scipy.special.erf(pre * (1.0 / math.sqrt(2.0))))
    return cdf + pre * jnp.exp(-0.5 * pre * pre) * (1.0 / math.sqrt(2.0 * math.pi))


def swap(value, axis, size, bits):
    return lax.ppermute(value, axis, [(i, i ^ bits) for i in range(size)])


def rows_at(value, start, count):
    return lax.dynamic_slice_in_dim(value, start, count, 0)


def dot(a, b, dims=((1,), (0,))):
    return lax.dot_general(a, b, (dims, ((), ())), preferred_element_type=F32)


def weight_kernel(scale, rows, groups, *refs):
    out = refs[-1]
    hidden = out.shape[1]
    tile = 256

    @pl.loop(0, hidden // tile)
    def _(step):
        cols = pl.ds(pl.multiple_of(step * tile, tile), tile)
        total = None
        for (left, first), pieces in groups:
            tokens = [refs[i][start : start + count, cols] for i, start, count in pieces]
            term = dot(refs[left][first : first + rows], jnp.concatenate(tokens, axis=0))
            total = term if total is None else total + term
        out[:, cols] = (total * scale).astype(BF)


def weight_term(refs, groups, scale, rows):
    hidden = refs[-1].shape[1]
    tokens = sum(count for _, pieces in groups for _, _, count in pieces)
    whole = pl.BlockSpec(memory_space=pltpu.VMEM)
    return pl.pallas_call(
        lambda *r: weight_kernel(scale, rows, groups, *r),
        out_shape=jax.ShapeDtypeStruct((rows, hidden), BF),
        in_specs=[pl.BlockSpec() if r.shape[1] != hidden else whole for r in refs],
        compiler_params=pltpu.CompilerParams(vmem_limit_bytes=8 * 1024 * 1024),
        cost_estimate=pl.CostEstimate(
            flops=2 * rows * tokens * hidden,
            bytes_accessed=2 * (rows * (tokens + hidden) + tokens * hidden),
            transcendentals=0,
        ),
    )(*refs)


Z = 16
ZH = Z // 2


def body(tokens_in, norm_gain, in_weight, cotangent):
    tok_rows, width = tokens_in.shape
    hidden = in_weight.shape[1]
    n_dp, n_mx, n_my = lax.axis_size("dp"), lax.axis_size("mx"), lax.axis_size("my")
    d_all = width * n_mx
    half = tok_rows // 2
    dp, my = lax.axis_index("dp"), lax.axis_index("my")
    core = lax.axis_index("mx") % 2
    x_lo, zl = dp // Z, dp % 2
    block = width // n_dp

    values = tokens_in.astype(F32)
    sum_one, sum_two = lax.psum((jnp.sum(values, axis=1), jnp.sum(values * values, axis=1)), "mx")
    row_mean = sum_one / d_all
    inv_std = lax.rsqrt(sum_two / d_all - row_mean * row_mean + epsilon)
    centred = (values - row_mean[:, None]) * inv_std[:, None]
    normed = (centred * norm_gain[None, :]).astype(BF)

    mine = rows_at(normed, core * half, half)
    other = rows_at(normed, (1 - core) * half, half)
    sent = dot(other, in_weight).astype(BF)
    from_core = swap(sent, "mx", n_mx, 1)
    kept = lax.optimization_barrier(dot(mine, in_weight)) + from_core.astype(F32)
    from_x = swap(kept.astype(BF), "mx", n_mx, 2)

    turned = jnp.concatenate([mine.T, other.T], axis=1).reshape(2, ZH, 2, block, tok_rows)
    columns = ZH * block

    def for_zl(index):
        return lax.dynamic_slice_in_dim(turned, index, 1, 2).reshape(2 * columns, tok_rows)

    here = for_zl(zl)
    near = swap(for_zl(1 - zl), "dp", n_dp, 1)
    from_x, near = lax.optimization_barrier((from_x, near))

    pre = kept + from_x.astype(F32)
    cot = rows_at(cotangent, core * half, half)
    dpre = (cot.astype(F32) * gelu_slope(pre)).astype(BF)

    def across(value, bits):
        n = n_dp * n_mx
        return lax.ppermute(value, ("dp", "mx"), [(i, i ^ (bits * n_mx + 2)) for i in range(n)])

    part = half // 2
    far = []
    for bits in (16, 17):
        far += [swap(dpre[:part], "dp", n_dp, bits), across(dpre[part:], bits)]
    near_dpre = swap(dpre, "dp", n_dp, 1)
    own_pair = swap(dpre, "mx", n_mx, 1)

    theirs = (1 - x_lo) * columns
    beyond = jnp.concatenate([rows_at(here, theirs, columns), rows_at(near, theirs, columns)], axis=0)
    beyond, own_pair = lax.optimization_barrier((beyond, own_pair))
    beyond = swap(beyond, "dp", n_dp, 16)
    own_rows = tok_rows // n_my
    right = [dpre, own_pair]
    in_order = jnp.where(core == 0, jnp.concatenate(right, axis=0), jnp.concatenate(right[::-1], axis=0))
    in_order = in_order.reshape(2, 2, 2, own_rows, hidden).transpose(2, 1, 0, 3, 4).reshape(tok_rows, hidden)
    keep = dot(in_order, in_weight, ((1,), (1,)))

    keep, near_dpre, *far = lax.optimization_barrier((keep, near_dpre, *far))
    far = jnp.concatenate(far, axis=0)
    far, beyond = lax.optimization_barrier((far, beyond))
    far_pair = swap(far, "mx", n_mx, 1)
    near_pair = swap(near_dpre, "mx", n_mx, 1)

    refs = [rows_at(here, x_lo * columns, columns), rows_at(near, x_lo * columns, columns), beyond]
    refs += [dpre, own_pair, near_dpre, near_pair, far, far_pair]
    groups = [
        ((0, 0), [(3, 0, half), (4, 0, half)]),
        ((1, 0), [(5, 0, half), (6, 0, half)]),
        ((2, 0), [(7, 0, half), (8, 0, half)]),
        ((2, columns), [(7, half, half), (8, half, half)]),
    ]
    term = weight_term(refs, groups, 1.0 / math.sqrt(n_dp * tok_rows), columns)
    teams = [[x * Z + h * 2 + l for h in range(ZH)] for x in range(2) for l in range(2)]
    grad_weight = lax.psum_scatter(
        term, "dp", scatter_dimension=0, axis_index_groups=teams, tiled=True
    ).reshape(1, 1, block, hidden)

    for bit in (1, 2, 4):
        rows = keep.shape[0] // 2
        mine_first = my // bit % 2 * rows
        give = rows_at(keep, rows - mine_first, rows).astype(BF)
        keep = rows_at(keep, mine_first, rows) + swap(give, "my", n_my, bit).astype(F32)
    dnormed = keep

    first_row = my * own_rows
    centred_rows = rows_at(centred, first_row, own_rows)
    inv_rows = rows_at(inv_std, first_row, own_rows)
    dcentred = dnormed * norm_gain[None, :]
    total_a, total_b = lax.psum(
        (jnp.sum(dcentred, axis=1), jnp.sum(dcentred * centred_rows, axis=1)), "mx"
    )
    grad_tokens = inv_rows[:, None] * (
        dcentred - total_a[:, None] / d_all - centred_rows * (total_b[:, None] / d_all)
    )
    return (grad_weight, grad_tokens.astype(BF))


def solution(mesh):
    return jax.shard_map(
        body,
        mesh=mesh,
        in_specs=(P("dp", "mx"), P("mx"), P("mx", "my"), P("dp", "my")),
        out_specs=(P("mx", "dp", None, "my"), P(("dp", "my"), "mx")),
        check_vma=False,
    )
```

```python
import math

import jax
import jax.numpy as jnp
from jax import lax
from jax.experimental import pallas as pl
from jax.experimental.pallas import tpu as pltpu
from jax.sharding import PartitionSpec as P

epsilon = 1e-06
BF = jnp.bfloat16
F32 = jnp.float32


def gelu_slope(pre):
    cdf = 0.5 * (1.0 + jax.scipy.special.erf(pre * (1.0 / math.sqrt(2.0))))
    return cdf + pre * jnp.exp(-0.5 * pre * pre) * (1.0 / math.sqrt(2.0 * math.pi))


def swap(value, axis, size, bits):
    return lax.ppermute(value, axis, [(i, i ^ bits) for i in range(size)])


def rows_at(value, start, count):
    return lax.dynamic_slice_in_dim(value, start, count, 0)


def dot(a, b, dims=((1,), (0,))):
    return lax.dot_general(a, b, (dims, ((), ())), preferred_element_type=F32)


def weight_kernel(scale, rows, *refs):
    left, right, out = refs[:2], refs[2:6], refs[6:]
    hidden = right[0].shape[1]
    tile = 256

    @pl.loop(0, hidden // tile)
    def _(step):
        cols = pl.ds(pl.multiple_of(step * tile, tile), tile)
        total = None
        for i in range(2):
            tokens = jnp.concatenate([right[2 * i][:, cols], right[2 * i + 1][:, cols]], axis=0)
            term = dot(left[i][...], tokens)
            total = term if total is None else total + term
        total = (total * scale).astype(BF)
        for i, ref in enumerate(out):
            ref[:, cols] = total[i * rows : (i + 1) * rows]


def weight_blocks(left, right, scale, rows):
    count = left[0].shape[0] // rows
    hidden = right[0].shape[1]
    tokens = sum(r.shape[0] for r in right)
    whole = pl.BlockSpec(memory_space=pltpu.VMEM)
    return pl.pallas_call(
        lambda *refs: weight_kernel(scale, rows, *refs),
        out_shape=[jax.ShapeDtypeStruct((rows, hidden), BF)] * count,
        in_specs=[whole] * (len(left) + len(right)),
        out_specs=[whole] * count,
        compiler_params=pltpu.CompilerParams(vmem_limit_bytes=8 * 1024 * 1024),
        cost_estimate=pl.CostEstimate(
            flops=2 * rows * count * tokens * hidden,
            bytes_accessed=2 * (rows * count * (tokens + hidden) + tokens * hidden),
            transcendentals=0,
        ),
    )(*left, *right)


Z = 16


def body(tokens_in, norm_gain, in_weight, cotangent):
    tok_rows, width = tokens_in.shape
    hidden = in_weight.shape[1]
    n_dp, n_mx, n_my = lax.axis_size("dp"), lax.axis_size("mx"), lax.axis_size("my")
    d_all = width * n_mx
    half = tok_rows // 2
    dp, my = lax.axis_index("dp"), lax.axis_index("my")
    core = lax.axis_index("mx") % 2
    z, x_lo = dp % Z, dp // Z
    block = width // n_dp

    values = tokens_in.astype(F32)
    sum_one, sum_two = lax.psum((jnp.sum(values, axis=1), jnp.sum(values * values, axis=1)), "mx")
    row_mean = sum_one / d_all
    inv_std = lax.rsqrt(sum_two / d_all - row_mean * row_mean + epsilon)
    centred = (values - row_mean[:, None]) * inv_std[:, None]
    normed = (centred * norm_gain[None, :]).astype(BF)

    mine = rows_at(normed, core * half, half)
    other = rows_at(normed, (1 - core) * half, half)
    sent = dot(other, in_weight).astype(BF)
    from_core = swap(sent, "mx", n_mx, 1)
    kept = lax.optimization_barrier(dot(mine, in_weight)) + from_core.astype(F32)
    from_x = swap(kept.astype(BF), "mx", n_mx, 2)

    turned = jnp.concatenate([mine.T, other.T], axis=1).reshape(2, Z, block, tok_rows)
    turned = jnp.concatenate([turned, turned], axis=1)

    def columns(index):
        piece = lax.dynamic_slice(turned, (index, z, 0, 0), (1, Z, block, tok_rows))
        return piece.reshape(Z * block, tok_rows)

    left = [columns(x_lo), swap(columns(1 - x_lo), "dp", n_dp, Z)]
    from_x, *left = lax.optimization_barrier((from_x, *left))

    pre = kept + from_x.astype(F32)
    cot = rows_at(cotangent, core * half, half)
    dpre = (cot.astype(F32) * gelu_slope(pre)).astype(BF)

    own_pair = swap(dpre, "mx", n_mx, 1)
    right = [dpre, own_pair]
    arrived = swap(dpre, "dp", n_dp, Z)

    in_order = jnp.where(core == 0, jnp.concatenate(right, axis=0), jnp.concatenate(right[::-1], axis=0))
    back = dot(in_order, in_weight, ((1,), (1,)))
    back, arrived = lax.optimization_barrier((back, arrived))
    dnormed = lax.psum_scatter(back, "my", scatter_dimension=0, tiled=True)
    own_rows = tok_rows // n_my

    right += [arrived, swap(arrived, "mx", n_mx, 1)]
    terms = weight_blocks(left, right, 1.0 / math.sqrt(n_dp * tok_rows), block)

    def hop(value, way):
        perm = [(i, i // Z * Z + (i + way) % Z) for i in range(n_dp)]
        return lax.ppermute(value.astype(BF), "dp", perm).astype(F32)

    ahead, behind = terms[Z // 2], terms[Z // 2 + 1]
    for step in range(1, Z // 2):
        ahead = hop(ahead, 1) + terms[Z // 2 - step].astype(F32)
        behind = hop(behind, -1) + terms[(Z // 2 + 1 + step) % Z].astype(F32)
    ahead, dnormed = lax.optimization_barrier((ahead, dnormed))
    grad_weight = (behind + hop(ahead, 1)).astype(BF).reshape(1, 1, block, hidden)

    first_row = my * own_rows
    centred_rows = rows_at(centred, first_row, own_rows)
    inv_rows = rows_at(inv_std, first_row, own_rows)
    dcentred = dnormed * norm_gain[None, :]
    total_a, total_b = lax.psum(
        (jnp.sum(dcentred, axis=1), jnp.sum(dcentred * centred_rows, axis=1)), "mx"
    )
    grad_tokens = inv_rows[:, None] * (
        dcentred - total_a[:, None] / d_all - centred_rows * (total_b[:, None] / d_all)
    )
    return (grad_weight, grad_tokens.astype(BF))


def solution(mesh):
    return jax.shard_map(
        body,
        mesh=mesh,
        in_specs=(P("dp", "mx"), P("mx"), P("mx", "my"), P("dp", "my")),
        out_specs=(P("mx", "dp", None, "my"), P(("dp", "my"), "mx")),
        check_vma=False,
    )
```

```python
import math

import jax
import jax.numpy as jnp
from jax import lax
from jax.experimental import pallas as pl
from jax.experimental.pallas import tpu as pltpu
from jax.sharding import PartitionSpec as P

epsilon = 1e-06
BF = jnp.bfloat16
F32 = jnp.float32


def gelu_slope(pre):
    cdf = 0.5 * (1.0 + jax.scipy.special.erf(pre * (1.0 / math.sqrt(2.0))))
    return cdf + pre * jnp.exp(-0.5 * pre * pre) * (1.0 / math.sqrt(2.0 * math.pi))


def swap(value, axis, size, bits):
    return lax.ppermute(value, axis, [(i, i ^ bits) for i in range(size)])


def rows_at(value, start, count):
    return lax.dynamic_slice_in_dim(value, start, count, 0)


def dot(a, b, dims=((1,), (0,))):
    return lax.dot_general(a, b, (dims, ((), ())), preferred_element_type=F32)


def weight_kernel(scale, rows, *refs):
    left, right, out = refs[:4], refs[4:12], refs[12:]
    hidden = right[0].shape[1]
    tile = 256

    @pl.loop(0, hidden // tile)
    def _(step):
        cols = pl.ds(pl.multiple_of(step * tile, tile), tile)
        total = None
        for i in range(4):
            tokens = jnp.concatenate([right[2 * i][:, cols], right[2 * i + 1][:, cols]], axis=0)
            term = dot(left[i][...], tokens)
            total = term if total is None else total + term
        total = (total * scale).astype(BF)
        for i, ref in enumerate(out):
            ref[:, cols] = total[i * rows : (i + 1) * rows]


def weight_blocks(left, right, scale, rows):
    count = left[0].shape[0] // rows
    hidden = right[0].shape[1]
    tokens = sum(r.shape[0] for r in right)
    whole = pl.BlockSpec(memory_space=pltpu.VMEM)
    return pl.pallas_call(
        lambda *refs: weight_kernel(scale, rows, *refs),
        out_shape=[jax.ShapeDtypeStruct((rows, hidden), BF)] * count,
        in_specs=[whole] * (len(left) + len(right)),
        out_specs=[whole] * count,
        compiler_params=pltpu.CompilerParams(vmem_limit_bytes=8 * 1024 * 1024),
        cost_estimate=pl.CostEstimate(
            flops=2 * rows * count * tokens * hidden,
            bytes_accessed=2 * (rows * count * (tokens + hidden) + tokens * hidden),
            transcendentals=0,
        ),
    )(*left, *right)


Z = 16
ZH = Z // 2
GROUP = (16, 1, 17)


def body(tokens_in, norm_gain, in_weight, cotangent):
    tok_rows, width = tokens_in.shape
    hidden = in_weight.shape[1]
    n_dp, n_mx, n_my = lax.axis_size("dp"), lax.axis_size("mx"), lax.axis_size("my")
    d_all = width * n_mx
    half = tok_rows // 2
    dp, my = lax.axis_index("dp"), lax.axis_index("my")
    core = lax.axis_index("mx") % 2
    zh, x_lo, zl = (dp % Z) // 2, dp // Z, dp % 2
    block = width // n_dp

    values = tokens_in.astype(F32)
    sum_one, sum_two = lax.psum((jnp.sum(values, axis=1), jnp.sum(values * values, axis=1)), "mx")
    row_mean = sum_one / d_all
    inv_std = lax.rsqrt(sum_two / d_all - row_mean * row_mean + epsilon)
    centred = (values - row_mean[:, None]) * inv_std[:, None]
    normed = (centred * norm_gain[None, :]).astype(BF)

    mine = rows_at(normed, core * half, half)
    other = rows_at(normed, (1 - core) * half, half)
    sent = dot(other, in_weight).astype(BF)
    from_core = swap(sent, "mx", n_mx, 1)
    kept = lax.optimization_barrier(dot(mine, in_weight)) + from_core.astype(F32)
    from_x = swap(kept.astype(BF), "mx", n_mx, 2)

    turned = jnp.concatenate([mine.T, other.T], axis=1).reshape(2, ZH, 2, block, tok_rows)
    turned = jnp.concatenate([turned, turned], axis=1)

    def columns(xb, zb):
        piece = lax.dynamic_slice(
            turned, (x_lo ^ xb, zh, zl ^ zb, 0, 0), (1, ZH, 1, block, tok_rows)
        )
        return piece.reshape(ZH * block, tok_rows)

    left = [columns(0, 0)]
    for bits in GROUP:
        left.append(swap(columns(bits // 16, bits % 2), "dp", n_dp, bits))
    from_x, *left = lax.optimization_barrier((from_x, *left))

    pre = kept + from_x.astype(F32)
    cot = rows_at(cotangent, core * half, half)
    dpre = (cot.astype(F32) * gelu_slope(pre)).astype(BF)

    own_pair = swap(dpre, "mx", n_mx, 1)
    right = [dpre, own_pair]
    arrived = [swap(dpre, "dp", n_dp, bits) for bits in GROUP]

    in_order = jnp.where(core == 0, jnp.concatenate(right, axis=0), jnp.concatenate(right[::-1], axis=0))
    back = dot(in_order, in_weight, ((1,), (1,)))
    back, arrived[1] = lax.optimization_barrier((back, arrived[1]))
    dnormed = lax.psum_scatter(back, "my", scatter_dimension=0, tiled=True)
    own_rows = tok_rows // n_my

    for piece in arrived:
        right += [piece, swap(piece, "mx", n_mx, 1)]
    terms = weight_blocks(left, right, 1.0 / math.sqrt(n_dp * tok_rows), block)

    def hop(value, way):
        perm = [(i, i // Z * Z + (i + 2 * way) % Z) for i in range(n_dp)]
        return lax.ppermute(value.astype(BF), "dp", perm).astype(F32)

    ahead, behind = terms[ZH // 2], terms[ZH // 2 + 1]
    for step in range(1, ZH // 2):
        ahead = hop(ahead, 1) + terms[ZH // 2 - step].astype(F32)
        behind = hop(behind, -1) + terms[(ZH // 2 + 1 + step) % ZH].astype(F32)
    ahead, dnormed = lax.optimization_barrier((ahead, dnormed))
    grad_weight = (behind + hop(ahead, 1)).astype(BF).reshape(1, 1, block, hidden)

    first_row = my * own_rows
    centred_rows = rows_at(centred, first_row, own_rows)
    inv_rows = rows_at(inv_std, first_row, own_rows)
    dcentred = dnormed * norm_gain[None, :]
    total_a, total_b = lax.psum(
        (jnp.sum(dcentred, axis=1), jnp.sum(dcentred * centred_rows, axis=1)), "mx"
    )
    grad_tokens = inv_rows[:, None] * (
        dcentred - total_a[:, None] / d_all - centred_rows * (total_b[:, None] / d_all)
    )
    return (grad_weight, grad_tokens.astype(BF))


def solution(mesh):
    return jax.shard_map(
        body,
        mesh=mesh,
        in_specs=(P("dp", "mx"), P("mx"), P("mx", "my"), P("dp", "my")),
        out_specs=(P("mx", "dp", None, "my"), P(("dp", "my"), "mx")),
        check_vma=False,
    )
```

```python
import math

import jax
import jax.numpy as jnp
from jax import lax
from jax.experimental import pallas as pl
from jax.experimental.pallas import tpu as pltpu
from jax.sharding import PartitionSpec as P

epsilon = 1e-06
BF = jnp.bfloat16
F32 = jnp.float32


def gelu_slope(pre):
    cdf = 0.5 * (1.0 + jax.scipy.special.erf(pre * (1.0 / math.sqrt(2.0))))
    return cdf + pre * jnp.exp(-0.5 * pre * pre) * (1.0 / math.sqrt(2.0 * math.pi))


def swap(value, axis, size, bits):
    return lax.ppermute(value, axis, [(i, i ^ bits) for i in range(size)])


def rows_at(value, start, count):
    return lax.dynamic_slice_in_dim(value, start, count, 0)


def dot(a, b, dims=((1,), (0,))):
    return lax.dot_general(a, b, (dims, ((), ())), preferred_element_type=F32)


def weight_kernel(scale, rows, *refs):
    left, right, out = refs[:4], refs[4:12], refs[12:]
    hidden = right[0].shape[1]
    tile = 256

    @pl.loop(0, hidden // tile)
    def _(step):
        cols = pl.ds(pl.multiple_of(step * tile, tile), tile)
        total = None
        for i in range(4):
            tokens = jnp.concatenate([right[2 * i][:, cols], right[2 * i + 1][:, cols]], axis=0)
            term = dot(left[i][...], tokens)
            total = term if total is None else total + term
        total = (total * scale).astype(BF)
        for i, ref in enumerate(out):
            ref[:, cols] = total[i * rows : (i + 1) * rows]


def weight_blocks(left, right, scale, rows):
    count = left[0].shape[0] // rows
    hidden = right[0].shape[1]
    tokens = sum(r.shape[0] for r in right)
    whole = pl.BlockSpec(memory_space=pltpu.VMEM)
    return pl.pallas_call(
        lambda *refs: weight_kernel(scale, rows, *refs),
        out_shape=[jax.ShapeDtypeStruct((rows, hidden), BF)] * count,
        in_specs=[whole] * (len(left) + len(right)),
        out_specs=[whole] * count,
        compiler_params=pltpu.CompilerParams(vmem_limit_bytes=8 * 1024 * 1024),
        cost_estimate=pl.CostEstimate(
            flops=2 * rows * count * tokens * hidden,
            bytes_accessed=2 * (rows * count * (tokens + hidden) + tokens * hidden),
            transcendentals=0,
        ),
    )(*left, *right)


Z = 16
ZH = Z // 2
GROUP = (16, 1, 17)


def body(tokens_in, norm_gain, in_weight, cotangent):
    tok_rows, width = tokens_in.shape
    hidden = in_weight.shape[1]
    n_dp, n_mx, n_my = lax.axis_size("dp"), lax.axis_size("mx"), lax.axis_size("my")
    d_all = width * n_mx
    half = tok_rows // 2
    dp, my = lax.axis_index("dp"), lax.axis_index("my")
    core = lax.axis_index("mx") % 2
    zh, x_lo, zl = (dp % Z) // 2, dp // Z, dp % 2
    block = width // n_dp

    values = tokens_in.astype(F32)
    sum_one, sum_two = lax.psum((jnp.sum(values, axis=1), jnp.sum(values * values, axis=1)), "mx")
    row_mean = sum_one / d_all
    inv_std = lax.rsqrt(sum_two / d_all - row_mean * row_mean + epsilon)
    centred = (values - row_mean[:, None]) * inv_std[:, None]
    normed = (centred * norm_gain[None, :]).astype(BF)

    mine = rows_at(normed, core * half, half)
    other = rows_at(normed, (1 - core) * half, half)
    sent = dot(other, in_weight).astype(BF)
    from_core = swap(sent, "mx", n_mx, 1)
    kept = lax.optimization_barrier(dot(mine, in_weight)) + from_core.astype(F32)
    from_x = swap(kept.astype(BF), "mx", n_mx, 2)

    turned = jnp.concatenate([mine.T, other.T], axis=1).reshape(2, ZH, 2, block, tok_rows)
    turned = jnp.concatenate([turned, turned], axis=1)

    def columns(xb, zb):
        piece = lax.dynamic_slice(
            turned, (x_lo ^ xb, zh, zl ^ zb, 0, 0), (1, ZH, 1, block, tok_rows)
        )
        return piece.reshape(ZH * block, tok_rows)

    left = [columns(0, 0)]
    for bits in GROUP:
        left.append(columns(bits // 16, bits % 2))
    left[2:] = [swap(piece, "dp", n_dp, bits) for piece, bits in zip(left[2:], GROUP[1:])]
    from_x, *left = lax.optimization_barrier((from_x, *left))

    pre = kept + from_x.astype(F32)
    cot = rows_at(cotangent, core * half, half)
    dpre = (cot.astype(F32) * gelu_slope(pre)).astype(BF)

    own_pair = swap(dpre, "mx", n_mx, 1)
    right = [dpre, own_pair]
    arrived = [swap(dpre, "dp", n_dp, bits) for bits in GROUP]

    in_order = jnp.where(core == 0, jnp.concatenate(right, axis=0), jnp.concatenate(right[::-1], axis=0))
    back = dot(in_order, in_weight, ((1,), (1,)))
    back, left[1] = lax.optimization_barrier((back, left[1]))
    left[1] = swap(left[1], "dp", n_dp, GROUP[0])
    left[1], arrived[1] = lax.optimization_barrier((left[1], arrived[1]))
    dnormed = lax.psum_scatter(back, "my", scatter_dimension=0, tiled=True)
    own_rows = tok_rows // n_my

    for piece in arrived:
        right += [piece, swap(piece, "mx", n_mx, 1)]
    terms = weight_blocks(left, right, 1.0 / math.sqrt(n_dp * tok_rows), block)

    def hop(value, way):
        perm = [(i, i // Z * Z + (i + 2 * way) % Z) for i in range(n_dp)]
        return lax.ppermute(value.astype(BF), "dp", perm).astype(F32)

    ahead, behind = terms[ZH // 2], terms[ZH // 2 + 1]
    for step in range(1, ZH // 2):
        ahead = hop(ahead, 1) + terms[ZH // 2 - step].astype(F32)
        behind = hop(behind, -1) + terms[(ZH // 2 + 1 + step) % ZH].astype(F32)
    ahead, dnormed = lax.optimization_barrier((ahead, dnormed))
    grad_weight = (behind + hop(ahead, 1)).astype(BF).reshape(1, 1, block, hidden)

    first_row = my * own_rows
    centred_rows = rows_at(centred, first_row, own_rows)
    inv_rows = rows_at(inv_std, first_row, own_rows)
    dcentred = dnormed * norm_gain[None, :]
    total_a, total_b = lax.psum(
        (jnp.sum(dcentred, axis=1), jnp.sum(dcentred * centred_rows, axis=1)), "mx"
    )
    grad_tokens = inv_rows[:, None] * (
        dcentred - total_a[:, None] / d_all - centred_rows * (total_b[:, None] / d_all)
    )
    return (grad_weight, grad_tokens.astype(BF))


def solution(mesh):
    return jax.shard_map(
        body,
        mesh=mesh,
        in_specs=(P("dp", "mx"), P("mx"), P("mx", "my"), P("dp", "my")),
        out_specs=(P("mx", "dp", None, "my"), P(("dp", "my"), "mx")),
        check_vma=False,
    )
```

```python
import math

import jax
import jax.numpy as jnp
from jax import lax
from jax.experimental import pallas as pl
from jax.experimental.pallas import tpu as pltpu
from jax.sharding import PartitionSpec as P

epsilon = 1e-06
BF = jnp.bfloat16
F32 = jnp.float32


def gelu_slope(pre):
    cdf = 0.5 * (1.0 + jax.scipy.special.erf(pre * (1.0 / math.sqrt(2.0))))
    return cdf + pre * jnp.exp(-0.5 * pre * pre) * (1.0 / math.sqrt(2.0 * math.pi))


def swap(value, axis, size, bits):
    return lax.ppermute(value, axis, [(i, i ^ bits) for i in range(size)])


def rows_at(value, start, count):
    return lax.dynamic_slice_in_dim(value, start, count, 0)


def dot(a, b, dims=((1,), (0,))):
    return lax.dot_general(a, b, (dims, ((), ())), preferred_element_type=F32)


def weight_kernel(scale, rows, *refs):
    left, right, out = refs[:4], refs[4:12], refs[12:]
    hidden = right[0].shape[1]
    tile = 256

    @pl.loop(0, hidden // tile)
    def _(step):
        cols = pl.ds(pl.multiple_of(step * tile, tile), tile)
        total = None
        for i in range(4):
            tokens = jnp.concatenate([right[2 * i][:, cols], right[2 * i + 1][:, cols]], axis=0)
            term = dot(left[i][...], tokens)
            total = term if total is None else total + term
        total = (total * scale).astype(BF)
        for i, ref in enumerate(out):
            ref[:, cols] = total[i * rows : (i + 1) * rows]


def weight_blocks(left, right, scale, rows):
    count = left[0].shape[0] // rows
    hidden = right[0].shape[1]
    tokens = sum(r.shape[0] for r in right)
    whole = pl.BlockSpec(memory_space=pltpu.VMEM)
    return pl.pallas_call(
        lambda *refs: weight_kernel(scale, rows, *refs),
        out_shape=[jax.ShapeDtypeStruct((rows, hidden), BF)] * count,
        in_specs=[whole] * (len(left) + len(right)),
        out_specs=[whole] * count,
        compiler_params=pltpu.CompilerParams(vmem_limit_bytes=8 * 1024 * 1024),
        cost_estimate=pl.CostEstimate(
            flops=2 * rows * count * tokens * hidden,
            bytes_accessed=2 * (rows * count * (tokens + hidden) + tokens * hidden),
            transcendentals=0,
        ),
    )(*left, *right)


Z = 16
ZH = Z // 2
GROUP = (16, 1, 17)


def body(tokens_in, norm_gain, in_weight, cotangent):
    tok_rows, width = tokens_in.shape
    hidden = in_weight.shape[1]
    n_dp, n_mx, n_my = lax.axis_size("dp"), lax.axis_size("mx"), lax.axis_size("my")
    d_all = width * n_mx
    half = tok_rows // 2
    dp, my = lax.axis_index("dp"), lax.axis_index("my")
    core = lax.axis_index("mx") % 2
    zh, x_lo, zl = (dp % Z) // 2, dp // Z, dp % 2
    block = width // n_dp

    values = tokens_in.astype(F32)
    sum_one, sum_two = lax.psum((jnp.sum(values, axis=1), jnp.sum(values * values, axis=1)), "mx")
    row_mean = sum_one / d_all
    inv_std = lax.rsqrt(sum_two / d_all - row_mean * row_mean + epsilon)
    centred = (values - row_mean[:, None]) * inv_std[:, None]
    normed = (centred * norm_gain[None, :]).astype(BF)

    mine = rows_at(normed, core * half, half)
    other = rows_at(normed, (1 - core) * half, half)
    sent = dot(other, in_weight).astype(BF)
    from_core = swap(sent, "mx", n_mx, 1)
    kept = lax.optimization_barrier(dot(mine, in_weight)) + from_core.astype(F32)
    from_x = swap(kept.astype(BF), "mx", n_mx, 2)

    turned = jnp.concatenate([mine.T, other.T], axis=1).reshape(2, ZH, 2, block, tok_rows)
    turned = jnp.concatenate([turned, turned], axis=1)

    def columns(xb, zb):
        piece = lax.dynamic_slice(
            turned, (x_lo ^ xb, zh, zl ^ zb, 0, 0), (1, ZH, 1, block, tok_rows)
        )
        return piece.reshape(ZH * block, tok_rows)

    left = [columns(0, 0)]
    for bits in GROUP:
        left.append(columns(bits // 16, bits % 2))
    left[2:] = [swap(piece, "dp", n_dp, bits) for piece, bits in zip(left[2:], GROUP[1:])]
    from_x, *left = lax.optimization_barrier((from_x, *left))

    pre = kept + from_x.astype(F32)
    cot = rows_at(cotangent, core * half, half)
    dpre = (cot.astype(F32) * gelu_slope(pre)).astype(BF)

    own_pair = swap(dpre, "mx", n_mx, 1)
    own_pair, left[1] = lax.optimization_barrier((own_pair, left[1]))
    left[1] = swap(left[1], "dp", n_dp, GROUP[0])
    right = [dpre, own_pair]
    arrived = [swap(dpre, "dp", n_dp, bits) for bits in GROUP]

    in_order = jnp.where(core == 0, jnp.concatenate(right, axis=0), jnp.concatenate(right[::-1], axis=0))
    back = dot(in_order, in_weight, ((1,), (1,)))
    back, arrived[2] = lax.optimization_barrier((back, arrived[2]))
    left[1], arrived[1] = lax.optimization_barrier((left[1], arrived[1]))
    dnormed = lax.psum_scatter(back, "my", scatter_dimension=0, tiled=True)
    own_rows = tok_rows // n_my

    for piece in arrived:
        right += [piece, swap(piece, "mx", n_mx, 1)]
    terms = weight_blocks(left, right, 1.0 / math.sqrt(n_dp * tok_rows), block)

    def hop(value, way):
        perm = [(i, i // Z * Z + (i + 2 * way) % Z) for i in range(n_dp)]
        return lax.ppermute(value.astype(BF), "dp", perm).astype(F32)

    ahead, behind = terms[ZH // 2], terms[ZH // 2 + 1]
    for step in range(1, ZH // 2):
        ahead = hop(ahead, 1) + terms[ZH // 2 - step].astype(F32)
        behind = hop(behind, -1) + terms[(ZH // 2 + 1 + step) % ZH].astype(F32)
    ahead, dnormed = lax.optimization_barrier((ahead, dnormed))
    grad_weight = (behind + hop(ahead, 1)).astype(BF).reshape(1, 1, block, hidden)

    first_row = my * own_rows
    centred_rows = rows_at(centred, first_row, own_rows)
    inv_rows = rows_at(inv_std, first_row, own_rows)
    dcentred = dnormed * norm_gain[None, :]
    total_a, total_b = lax.psum(
        (jnp.sum(dcentred, axis=1), jnp.sum(dcentred * centred_rows, axis=1)), "mx"
    )
    grad_tokens = inv_rows[:, None] * (
        dcentred - total_a[:, None] / d_all - centred_rows * (total_b[:, None] / d_all)
    )
    return (grad_weight, grad_tokens.astype(BF))


def solution(mesh):
    return jax.shard_map(
        body,
        mesh=mesh,
        in_specs=(P("dp", "mx"), P("mx"), P("mx", "my"), P("dp", "my")),
        out_specs=(P("mx", "dp", None, "my"), P(("dp", "my"), "mx")),
        check_vma=False,
    )
```

```python
import math

import jax
import jax.numpy as jnp
from jax import lax
from jax.experimental import pallas as pl
from jax.experimental.pallas import tpu as pltpu
from jax.sharding import PartitionSpec as P

epsilon = 1e-06
BF = jnp.bfloat16
F32 = jnp.float32


def gelu_slope(pre):
    cdf = 0.5 * (1.0 + jax.scipy.special.erf(pre * (1.0 / math.sqrt(2.0))))
    return cdf + pre * jnp.exp(-0.5 * pre * pre) * (1.0 / math.sqrt(2.0 * math.pi))


def swap(value, axis, size, bits):
    return lax.ppermute(value, axis, [(i, i ^ bits) for i in range(size)])


def rows_at(value, start, count):
    return lax.dynamic_slice_in_dim(value, start, count, 0)


def dot(a, b, dims=((1,), (0,))):
    return lax.dot_general(a, b, (dims, ((), ())), preferred_element_type=F32)


def weight_kernel(scale, rows, *refs):
    left, right, out = refs[:4], refs[4:12], refs[12:]
    hidden = right[0].shape[1]
    tile = 256

    @pl.loop(0, hidden // tile)
    def _(step):
        cols = pl.ds(pl.multiple_of(step * tile, tile), tile)
        total = None
        for i in range(4):
            tokens = jnp.concatenate([right[2 * i][:, cols], right[2 * i + 1][:, cols]], axis=0)
            term = dot(left[i][...], tokens)
            total = term if total is None else total + term
        total = (total * scale).astype(BF)
        for i, ref in enumerate(out):
            ref[:, cols] = total[i * rows : (i + 1) * rows]


def weight_blocks(left, right, scale, rows):
    count = left[0].shape[0] // rows
    hidden = right[0].shape[1]
    tokens = sum(r.shape[0] for r in right)
    whole = pl.BlockSpec(memory_space=pltpu.VMEM)
    return pl.pallas_call(
        lambda *refs: weight_kernel(scale, rows, *refs),
        out_shape=[jax.ShapeDtypeStruct((rows, hidden), BF)] * count,
        in_specs=[whole] * (len(left) + len(right)),
        out_specs=[whole] * count,
        compiler_params=pltpu.CompilerParams(vmem_limit_bytes=8 * 1024 * 1024),
        cost_estimate=pl.CostEstimate(
            flops=2 * rows * count * tokens * hidden,
            bytes_accessed=2 * (rows * count * (tokens + hidden) + tokens * hidden),
            transcendentals=0,
        ),
    )(*left, *right)


Z = 16
ZH = Z // 2
GROUP = (16, 1, 17)


def body(tokens_in, norm_gain, in_weight, cotangent):
    tok_rows, width = tokens_in.shape
    hidden = in_weight.shape[1]
    n_dp, n_mx, n_my = lax.axis_size("dp"), lax.axis_size("mx"), lax.axis_size("my")
    d_all = width * n_mx
    half = tok_rows // 2
    dp, my = lax.axis_index("dp"), lax.axis_index("my")
    core = lax.axis_index("mx") % 2
    zh, x_lo, zl = (dp % Z) // 2, dp // Z, dp % 2
    block = width // n_dp

    values = tokens_in.astype(F32)
    sum_one, sum_two = lax.psum((jnp.sum(values, axis=1), jnp.sum(values * values, axis=1)), "mx")
    row_mean = sum_one / d_all
    inv_std = lax.rsqrt(sum_two / d_all - row_mean * row_mean + epsilon)
    centred = (values - row_mean[:, None]) * inv_std[:, None]
    normed = (centred * norm_gain[None, :]).astype(BF)

    mine = rows_at(normed, core * half, half)
    other = rows_at(normed, (1 - core) * half, half)
    sent = dot(other, in_weight).astype(BF)
    from_core = swap(sent, "mx", n_mx, 1)
    kept = lax.optimization_barrier(dot(mine, in_weight)) + from_core.astype(F32)
    from_x = swap(kept.astype(BF), "mx", n_mx, 2)

    turned = jnp.concatenate([mine.T, other.T], axis=1).reshape(2, ZH, 2, block, tok_rows)
    turned = jnp.concatenate([turned, turned], axis=1)

    def columns(xb, zb):
        piece = lax.dynamic_slice(
            turned, (x_lo ^ xb, zh, zl ^ zb, 0, 0), (1, ZH, 1, block, tok_rows)
        )
        return piece.reshape(ZH * block, tok_rows)

    left = [columns(0, 0)]
    for bits in GROUP:
        left.append(columns(bits // 16, bits % 2))
    left[2:] = [swap(piece, "dp", n_dp, bits) for piece, bits in zip(left[2:], GROUP[1:])]
    from_x, *left = lax.optimization_barrier((from_x, *left))

    pre = kept + from_x.astype(F32)
    cot = rows_at(cotangent, core * half, half)
    dpre = (cot.astype(F32) * gelu_slope(pre)).astype(BF)

    own_pair = swap(dpre, "mx", n_mx, 1)
    own_pair, left[1] = lax.optimization_barrier((own_pair, left[1]))
    left[1] = swap(left[1], "dp", n_dp, GROUP[0])
    right = [dpre, own_pair]
    later, own_pair = lax.optimization_barrier((dpre, own_pair))
    arrived = [swap(dpre if bits == 1 else later, "dp", n_dp, bits) for bits in GROUP]

    in_order = jnp.where(core == 0, jnp.concatenate(right, axis=0), jnp.concatenate(right[::-1], axis=0))
    back = dot(in_order, in_weight, ((1,), (1,)))
    back, arrived[2] = lax.optimization_barrier((back, arrived[2]))
    left[1], arrived[1] = lax.optimization_barrier((left[1], arrived[1]))
    dnormed = lax.psum_scatter(back, "my", scatter_dimension=0, tiled=True)
    own_rows = tok_rows // n_my

    for piece in arrived:
        right += [piece, swap(piece, "mx", n_mx, 1)]
    terms = weight_blocks(left, right, 1.0 / math.sqrt(n_dp * tok_rows), block)

    def hop(value, way):
        perm = [(i, i // Z * Z + (i + 2 * way) % Z) for i in range(n_dp)]
        return lax.ppermute(value.astype(BF), "dp", perm).astype(F32)

    ahead, behind = terms[ZH // 2], terms[ZH // 2 + 1]
    for step in range(1, ZH // 2):
        ahead = hop(ahead, 1) + terms[ZH // 2 - step].astype(F32)
        behind = hop(behind, -1) + terms[(ZH // 2 + 1 + step) % ZH].astype(F32)
    ahead, dnormed = lax.optimization_barrier((ahead, dnormed))
    grad_weight = (behind + hop(ahead, 1)).astype(BF).reshape(1, 1, block, hidden)

    first_row = my * own_rows
    centred_rows = rows_at(centred, first_row, own_rows)
    inv_rows = rows_at(inv_std, first_row, own_rows)
    dcentred = dnormed * norm_gain[None, :]
    total_a, total_b = lax.psum(
        (jnp.sum(dcentred, axis=1), jnp.sum(dcentred * centred_rows, axis=1)), "mx"
    )
    grad_tokens = inv_rows[:, None] * (
        dcentred - total_a[:, None] / d_all - centred_rows * (total_b[:, None] / d_all)
    )
    return (grad_weight, grad_tokens.astype(BF))


def solution(mesh):
    return jax.shard_map(
        body,
        mesh=mesh,
        in_specs=(P("dp", "mx"), P("mx"), P("mx", "my"), P("dp", "my")),
        out_specs=(P("mx", "dp", None, "my"), P(("dp", "my"), "mx")),
        check_vma=False,
    )
```
